32 devices in a mesh: dp: 16 (over z, y, core), tensor: 2 (over x).
Axes of the slice: x: 2, y: 2, z: 4, core: 2. Of those that a mesh axis runs over, the one named last changes fastest.
Arguments:
- tokens: bfloat16 [2, 12288, 512], P(None, 'dp'), may hold values from -6 to 6
- lengths: int32 [2, 1536], P(None, 'dp'), may hold values from 1 to 8
- live_count: int32 [2], replicated, may hold values from 1152 to 1536
- cotangent: bfloat16 [2, 1536, 2048], P(None, 'dp', 'tensor'), may hold values from -6 to 6
- inflow: float32 [3, 512, 512], P(None, 'dp', 'tensor'), may hold values from -0.25 to 0.25
- outflow: float32 [512, 512], P('tensor', 'dp'), may hold values from -0.5 to 0.5
- expand: float32 [512, 2048], P('dp', 'tensor'), may hold values from -0.25 to 0.25
- shrink: float32 [2048, 512], P('tensor', 'dp'), may hold values from -0.125 to 0.125
- emitter: float32 [512, 2048], P('dp', 'tensor'), may hold values from -0.25 to 0.25
- inflow_prior: float32 [3, 512, 512], P(None, 'dp', 'tensor'), may hold values from -96 to 96
- outflow_prior: float32 [512, 512], P('tensor', 'dp'), may hold values from -192 to 192
- expand_prior: float32 [512, 2048], P('dp', 'tensor'), may hold values from -192 to 192
- shrink_prior: float32 [2048, 512], P('tensor', 'dp'), may hold values from -96 to 96
- emitter_prior: float32 [512, 2048], P('dp', 'tensor'), may hold values from -192 to 192
- vectors: float32 [6656], replicated, as said below
- vector_prior: float32 [6656], replicated, may hold values from -20 to 20
Outputs:
- emitted: bfloat16 [2, 1536, 2048], P(None, 'dp', 'tensor')
- token_grad: float32 [2, 12288, 512], P(None, 'dp')
- inflow_new: float32 [3, 512, 512], P(None, 'dp', 'tensor')
- outflow_new: float32 [512, 512], P('tensor', 'dp')
- expand_new: float32 [512, 2048], P('dp', 'tensor')
- shrink_new: float32 [2048, 512], P('tensor', 'dp')
- emitter_new: float32 [512, 2048], P('dp', 'tensor')
- inflow_velocity: float32 [3, 512, 512], P(None, 'dp', 'tensor')
- outflow_velocity: float32 [512, 512], P('tensor', 'dp')
- expand_velocity: float32 [512, 2048], P('dp', 'tensor')
- shrink_velocity: float32 [2048, 512], P('tensor', 'dp')
- emitter_velocity: float32 [512, 2048], P('dp', 'tensor')
- vector_new: float32 [6656], replicated
- vector_velocity: float32 [6656], replicated
The draws below stay inside these ranges and needn't reach their ends.
Inputs may be any that keep to these rules, and one draw needn't show every extreme that they name: The two norm gains in vectors are positive.
All inputs are finite; a program needn't handle non-finite values.
Results may differ from the reference program's by a relative error of at most 0.015.
Values may be sent and summed in bfloat16 or wider, within the bound.
No kernel may reach another device: no remote copies, remote signals or barrier semaphores. Data moves between devices by JAX's collectives and lax.ppermute only.
A program may use at most 192 MiB of HBM per device.

```python
import math
import jax
import jax.numpy as jnp
from jax import lax

D = 512
HEADS = 8
HEAD_DIM = 64
FF = 2048
OUT = 2048
S = 8
MICRO = 2
ENTRIES = 1536
NVEC = 6656


def draw_vectors(key, part):
    key = jax.random.fold_in(key, 11)
    first, second = jax.random.split(key)
    places = jnp.arange(5 * D + FF + OUT, dtype=jnp.int32)
    gains = jnp.exp(0.3 * jax.random.normal(first, places.shape, jnp.float32))
    shifts = 0.2 * jax.random.normal(second, places.shape, jnp.float32)
    is_gain = (places < D) | (places >= 2 * D) & (places < 3 * D)
    return jnp.where(is_gain, gains, shifts).astype(jnp.float32)


def place_ends(values, stream_key, low, top_value):
    dims = values.shape
    index_at = [jax.random.randint(jax.random.fold_in(stream_key, axis), (), 0, dims[axis]) for axis in range(len(dims))]
    values = values.at[tuple(index_at)].set(low)
    longest = dims.index(max(dims))
    index_at[longest] = (index_at[longest] + 1) % dims[longest]
    return values.at[tuple(index_at)].set(top_value)


def shard_levels(stream_key, dims, shards, least, high):
    loudness, own = 1.0, jax.random.fold_in(stream_key, 6)
    for position, blocks in shards:
        steps = jnp.exp(jax.random.uniform(jax.random.fold_in(own, position), (blocks,), jnp.float32, least / len(shards), high / len(shards)))
        loudness = loudness * jnp.repeat(steps, dims[position] // blocks).reshape([-1 if axis == position else 1 for axis in range(len(dims))])
    return loudness


def gaussian(own_key, dims, scale, bound, cuts=(), kind=jnp.bfloat16):
    array = jax.random.normal(own_key, dims, jnp.float32) * scale
    if len(cuts) > 0:
        array = shard_levels(own_key, dims, cuts, -0.22, 0.18) * array
    return jnp.clip(array, min=-bound, max=bound).astype(kind)


def setup_inputs(seed: int = 0) -> dict:
    key_of = jax.random.split(jax.random.key(seed), 17)
    return {
        "tokens": gaussian(key_of[0], (MICRO, ENTRIES * S, D), 1.0, 6.0, ((1, 16),)),
        "lengths": place_ends(jax.random.randint(key_of[1], (MICRO, ENTRIES), 1, S + 1), jax.random.fold_in(key_of[1], 1), 1, S).astype(jnp.int32),
        "live_count": jax.random.randint(key_of[2], (MICRO,), ENTRIES * 3 // 4, ENTRIES + 1).astype(jnp.int32),
        "cotangent": gaussian(key_of[3], (MICRO, ENTRIES, OUT), 1.0, 6.0, ((1, 16), (2, 2))),
        "inflow": gaussian(key_of[4], (3, D, D), D ** -0.5, 0.25, ((1, 16), (2, 2)), jnp.float32),
        "outflow": gaussian(key_of[5], (D, D), (D // 4) ** -0.5, 0.5, ((0, 2), (1, 16)), jnp.float32),
        "expand": gaussian(key_of[6], (D, FF), D ** -0.5, 0.25, ((0, 16), (1, 2)), jnp.float32),
        "shrink": gaussian(key_of[7], (FF, D), FF ** -0.5, 0.125, ((0, 2), (1, 16)), jnp.float32),
        "emitter": gaussian(key_of[8], (D, OUT), D ** -0.5, 0.25, ((0, 16), (1, 2)), jnp.float32),
        "inflow_prior": gaussian(key_of[9], (3, D, D), (0.1 * (MICRO * ENTRIES * S) ** 0.5), 96.0, ((1, 16), (2, 2)), jnp.float32),
        "outflow_prior": gaussian(key_of[10], (D, D), (0.2 * (MICRO * ENTRIES * S) ** 0.5), 192.0, ((0, 2), (1, 16)), jnp.float32),
        "expand_prior": gaussian(key_of[11], (D, FF), (0.2 * (MICRO * ENTRIES * S) ** 0.5), 192.0, ((0, 16), (1, 2)), jnp.float32),
        "shrink_prior": gaussian(key_of[12], (FF, D), (0.1 * (MICRO * ENTRIES * S) ** 0.5), 96.0, ((0, 2), (1, 16)), jnp.float32),
        "emitter_prior": gaussian(key_of[13], (D, OUT), (0.6 * (MICRO * ENTRIES) ** 0.5), 192.0, ((0, 16), (1, 2)), jnp.float32),
        "vectors": draw_vectors(jax.random.fold_in(key_of[16], 71), 0),
        "vector_prior": gaussian(key_of[15], (NVEC,), (0.02 * (MICRO * ENTRIES * S) ** 0.5), 20.0, (), jnp.float32),
    }


@jax.custom_vjp
def low(v):
    return lax.optimization_barrier(v.astype(jnp.bfloat16)).astype(jnp.float32)

@jax.custom_vjp
def low_back(v):
    return v

def low_keep(v):
    return (low(v), None)

def low_pass(kept, grad):
    return (grad,)

def back_keep(v):
    return (v, None)

def back_low(kept, grad):
    return (low(grad),)
low.defvjp(low_keep, low_pass)
low_back.defvjp(back_keep, back_low)
HIGH = lax.Precision.HIGHEST
norm_eps = 1e-05
coef_a = 3.4445
coef_b = -4.775
coef_c = 2.0315

def matmul(left, right):
    return jnp.dot(left, right, precision=HIGH, preferred_element_type=jnp.float32)

def normalize(value, gain, shift):
    centred = value - lax.optimization_barrier(jnp.mean(value, axis=-1, keepdims=True))
    return centred * lax.rsqrt(lax.optimization_barrier(jnp.mean(centred * centred, axis=-1, keepdims=True)) + norm_eps) * gain + shift

def orthogonal(matrix):
    rows, cols = matrix.shape
    work = matrix.T if rows > cols else matrix
    work = work / (jnp.sqrt(jnp.sum(work * work)) + 1e-07)
    for turn in range(5):
        gram = matmul(work, work.T)
        poly = coef_b * gram + coef_c * matmul(gram, gram)
        work = coef_a * work + matmul(poly, work)
    if rows > cols:
        work = work.T
    return work * math.sqrt(max(1.0, rows / cols))

def forward(tokens, lengths, inflow, outflow, expand, shrink, emitter, vectors):
    entries = lengths.shape[0]
    gain_a = vectors[0:D]
    shift_a = vectors[D:2 * D]
    gain_b = vectors[2 * D:3 * D]
    shift_b = vectors[3 * D:4 * D]
    bias_model = vectors[4 * D:5 * D]
    bias_hidden = vectors[5 * D:5 * D + FF]
    bias_out = vectors[5 * D + FF:5 * D + FF + OUT]
    low_in = low(inflow)
    low_out = low(outflow)
    low_expand = low(expand)
    low_shrink = low(shrink)
    low_emit = low(emitter)
    act = low(normalize(tokens, gain_a, shift_a))
    query = low(low_back(matmul(act, low_in[0]))).reshape(entries, S, HEADS, HEAD_DIM)
    keys = low(low_back(matmul(act, low_in[1]))).reshape(entries, S, HEADS, HEAD_DIM)
    values = low(low_back(matmul(act, low_in[2]))).reshape(entries, S, HEADS, HEAD_DIM)
    scores = low_back(jnp.einsum('eshd,ethd->ehst', query, keys, precision=HIGH) * HEAD_DIM ** (-0.5))
    live_slot = jnp.arange(S, dtype=jnp.int32)[None, :] < lengths[:, None]
    scores = jnp.where(live_slot[:, None, None, :], scores, -1e+30)
    probs = low(jax.nn.softmax(scores, axis=-1))
    mixed = low(low_back(jnp.einsum('ehst,ethd->eshd', probs, values, precision=HIGH))).reshape(entries * S, D)
    hidden = tokens + low_back(matmul(mixed, low_out))
    act_two = low(normalize(hidden, gain_b, shift_b))
    inner = low_back(matmul(act_two, low_expand) + bias_hidden)
    spread = low(jax.nn.gelu(inner, approximate=False))
    result = hidden + low_back(matmul(spread, low_shrink) + bias_model)
    slot_weight = live_slot.astype(jnp.float32) / lengths[:, None].astype(jnp.float32)
    pooled = lax.optimization_barrier(jnp.sum(result.reshape(entries, S, D) * slot_weight[:, :, None], axis=1))
    return matmul(low(pooled), low_emit) + bias_out

def reference(tokens, lengths, live_count, cotangent, inflow, outflow, expand, shrink, emitter, inflow_prior, outflow_prior, expand_prior, shrink_prior, emitter_prior, vectors, vector_prior):
    block = min(ENTRIES, 512)
    count = ENTRIES // block
    weights = (inflow, outflow, expand, shrink, emitter, vectors)
    totals = tuple((jnp.zeros_like(weight) for weight in weights))
    emitted_all = []
    token_all = []
    for batch_index in range(MICRO):
        token_blocks = tokens[batch_index].astype(jnp.float32).reshape(count, block * S, D)
        length_blocks = lengths[batch_index].reshape(count, block)
        cot_blocks = cotangent[batch_index].astype(jnp.float32).reshape(count, block, OUT)
        starts = jnp.arange(count, dtype=jnp.int32) * block
        limit = live_count[batch_index]

        def one_block(carry, item):
            token_block, length_block, cot_block, start = item
            alive = start + jnp.arange(block, dtype=jnp.int32) < limit
            cot_block = cot_block * alive[:, None].astype(jnp.float32)

            def local(tok, w_a, w_b, w_c, w_d, w_e, w_f):
                return forward(tok, length_block, w_a, w_b, w_c, w_d, w_e, w_f)
            value, pullback = jax.vjp(local, token_block, *weights)
            grads = pullback(cot_block)
            carry = tuple((total + grad for total, grad in zip(carry, grads[1:])))
            return (carry, (value.astype(jnp.bfloat16), grads[0]))
        totals, (out_blocks, grad_blocks) = lax.scan(one_block, totals, (token_blocks, length_blocks, cot_blocks, starts))
        emitted_all.append(out_blocks.reshape(ENTRIES, OUT))
        token_all.append(grad_blocks.reshape(ENTRIES * S, D))
    grad_in, grad_out, grad_expand, grad_shrink, grad_emit, grad_vec = totals
    inflow_velocity = 0.95 * inflow_prior + grad_in
    outflow_velocity = 0.95 * outflow_prior + grad_out
    expand_velocity = 0.95 * expand_prior + grad_expand
    shrink_velocity = 0.95 * shrink_prior + grad_shrink
    emitter_velocity = 0.95 * emitter_prior + grad_emit
    inflow_ortho = jnp.stack([orthogonal(inflow_velocity[0]), orthogonal(inflow_velocity[1]), orthogonal(inflow_velocity[2])])
    inflow_new = inflow - 0.6 * inflow_ortho
    outflow_new = outflow - 0.6 * orthogonal(outflow_velocity)
    expand_new = expand - 0.6 * orthogonal(expand_velocity)
    shrink_new = shrink - 0.6 * orthogonal(shrink_velocity)
    emitter_new = emitter - 0.6 * orthogonal(emitter_velocity)
    vector_velocity = 0.9 * vector_prior + grad_vec
    vector_new = vectors - 0.005 * vector_velocity
    return (jnp.stack(emitted_all), jnp.stack(token_all), inflow_new, outflow_new, expand_new, shrink_new, emitter_new, inflow_velocity, outflow_velocity, expand_velocity, shrink_velocity, emitter_velocity, vector_new, vector_velocity)
```

```python
import functools
import math

import jax
import jax.numpy as jnp
from jax import lax
from jax.experimental import pallas as pl
from jax.experimental.pallas import tpu as pltpu
from jax.sharding import PartitionSpec as P

D = 512
HEAD_DIM = 64
FF = 2048
OUT = 2048
S = 8
MICRO = 2
TILE = 128

norm_eps = 1e-05
coef_a = 3.4445
coef_b = -4.775
coef_c = 2.0315
f32 = jnp.float32
bf16 = jnp.bfloat16


def nn(left, right):
    return jnp.dot(left, right, preferred_element_type=f32)


def tn(left, right):
    return lax.dot_general(left, right, (((0,), (0,)), ((), ())), preferred_element_type=f32)


def nt(left, right):
    return lax.dot_general(left, right, (((1,), (1,)), ((), ())), preferred_element_type=f32)


def swap_tensor(x):
    return lax.ppermute(x, "tensor", [(0, 1), (1, 0)])


def swap_dp(x, mask):
    size = lax.axis_size("dp")
    return lax.ppermute(x, "dp", [(i, i ^ mask) for i in range(size)])


def dp_bits():
    return lax.axis_size("dp").bit_length() - 1


def bit_of(b):
    return (lax.axis_index("dp") >> b) & 1


def gather_step(cur, step):
    if step == "x":
        return jnp.concatenate([cur, swap_tensor(cur)], axis=0)
    recv = swap_dp(cur, 1 << step)
    mine_high = bit_of(step) == 1
    axis = cur.ndim - 2
    return jnp.where(
        mine_high, jnp.stack([recv, cur], axis=axis), jnp.stack([cur, recv], axis=axis)
    )


def gather_rows(cur, steps):
    for step in steps:
        cur = gather_step(cur, step)
    return cur


def halves_of(cur):
    cols = cur.shape[-1]
    return cur[0].reshape(-1, cols), cur[1].reshape(-1, cols)


def reduce_chunk(own, oth, order):
    bits = dp_bits()
    cols = own.shape[-1]
    rows = own.shape[0] >> bits

    def drop_bit(arr, b):
        axis = arr.ndim - 3
        send = lax.dynamic_index_in_dim(arr, 1 - bit_of(b), axis, keepdims=False)
        keep = lax.dynamic_index_in_dim(arr, bit_of(b), axis, keepdims=False)
        recv = swap_dp(send.astype(bf16), 1 << b)
        return keep.astype(f32) + recv.astype(f32)

    view = (2,) * bits + (rows, cols)
    own, oth = own.reshape(view), oth.reshape(view)
    for step in order:
        if step == "x":
            own = own.astype(f32) + swap_tensor(oth.astype(bf16)).astype(f32)
            oth = None
        else:
            own = drop_bit(own, step)
            oth = None if oth is None else drop_bit(oth, step)
        if step != order[-1]:
            own = own.astype(bf16)
            oth = None if oth is None else oth.astype(bf16)
    return own


def sum_everywhere(vec):
    for b in range(dp_bits()):
        vec = vec + swap_dp(vec, 1 << b)
    return vec + swap_tensor(vec)


def head_masks():
    lane = lax.broadcasted_iota(jnp.int32, (TILE, TILE), 1)
    return lane < HEAD_DIM


def slot_mask(live_ref):
    row = lax.broadcasted_iota(jnp.int32, (TILE, TILE), 0)
    col = lax.broadcasted_iota(jnp.int32, (TILE, TILE), 1)
    return jnp.logical_and(row // S == col // S, live_ref[0] > 0.0)


def probabilities(query, keys, valid):
    scores = nt(query, keys) * (HEAD_DIM**-0.5)
    scores = jnp.where(valid, scores, -1e30)
    top = jnp.max(scores, axis=1, keepdims=True)
    weight = jnp.exp(scores - top)
    return weight / jnp.sum(weight, axis=1, keepdims=True)


def attend_kernel(live_ref, own_ref, oth_ref, mixed_own_ref, mixed_oth_ref):
    valid = slot_mask(live_ref)
    first = head_masks()
    width = mixed_own_ref.shape[1]
    zero = jnp.zeros((TILE, TILE), bf16)
    for src, dst in ((own_ref, mixed_own_ref), (oth_ref, mixed_oth_ref)):
        for pair in range(width // TILE):
            at = pair * TILE
            q = src[:, at : at + TILE]
            k = src[:, width + at : width + at + TILE]
            v = src[:, 2 * width + at : 2 * width + at + TILE]
            total = jnp.zeros((TILE, TILE), f32)
            for take_first in (True, False):
                pick = functools.partial(pick_head, first, take_first, zero)
                probs = probabilities(pick(q), k, valid)
                total += nn(probs.astype(bf16), pick(v))
            dst[:, at : at + TILE] = total.astype(bf16)


def pick_head(first, take_first, zero, value):
    return jnp.where(first, value, zero) if take_first else jnp.where(first, zero, value)


def attend_back_kernel(
    live_ref, own_ref, oth_ref, d_own_ref, d_oth_ref, out_own_ref, out_oth_ref
):
    valid = slot_mask(live_ref)
    first = head_masks()
    width = d_own_ref.shape[1]
    zero = jnp.zeros((TILE, TILE), bf16)
    scale = HEAD_DIM**-0.5
    for src, grad, dst in (
        (own_ref, d_own_ref, out_own_ref),
        (oth_ref, d_oth_ref, out_oth_ref),
    ):
        for pair in range(width // TILE):
            at = pair * TILE
            q = src[:, at : at + TILE]
            k = src[:, width + at : width + at + TILE]
            v = src[:, 2 * width + at : 2 * width + at + TILE]
            g = grad[:, at : at + TILE]
            d_q = jnp.zeros((TILE, TILE), f32)
            d_k = jnp.zeros((TILE, TILE), f32)
            d_v = jnp.zeros((TILE, TILE), f32)
            for take_first in (True, False):
                pick = functools.partial(pick_head, first, take_first, zero)
                q_head, g_head = pick(q), pick(g)
                probs = probabilities(q_head, k, valid)
                d_probs = nt(g_head, v)
                inner = jnp.sum(probs * d_probs, axis=1, keepdims=True)
                d_scores = (probs * (d_probs - inner)).astype(bf16)
                d_v += tn(probs.astype(bf16), g_head)
                d_q += nn(d_scores, pick(k))
                d_k += tn(d_scores, q_head)
            dst[:, at : at + TILE] = (d_q * scale).astype(bf16)
            dst[:, width + at : width + at + TILE] = (d_k * scale).astype(bf16)
            dst[:, 2 * width + at : 2 * width + at + TILE] = d_v.astype(bf16)


def rows_spec(cols):
    return pl.BlockSpec((TILE, cols), lambda i: (i, 0))


def live_spec():
    return pl.BlockSpec((1, 1, TILE), lambda i: (i, 0, 0))


def attend(live, own, oth):
    rows, wide = own.shape
    width = wide // 3
    return pl.pallas_call(
        attend_kernel,
        grid=(rows // TILE,),
        in_specs=[live_spec(), rows_spec(wide), rows_spec(wide)],
        out_specs=[rows_spec(width), rows_spec(width)],
        out_shape=[jax.ShapeDtypeStruct((rows, width), bf16)] * 2,
    )(live, own, oth)


def attend_back(live, own, oth, d_own, d_oth):
    rows, wide = own.shape
    width = wide // 3
    return pl.pallas_call(
        attend_back_kernel,
        grid=(rows // TILE,),
        in_specs=[
            live_spec(),
            rows_spec(wide),
            rows_spec(wide),
            rows_spec(width),
            rows_spec(width),
        ],
        out_specs=[rows_spec(wide), rows_spec(wide)],
        out_shape=[jax.ShapeDtypeStruct((rows, wide), bf16)] * 2,
    )(live, own, oth, d_own, d_oth)


def norm_stats(value):
    centred = value - jnp.mean(value, axis=-1, keepdims=True)
    factor = lax.rsqrt(jnp.mean(centred * centred, axis=-1, keepdims=True) + norm_eps)
    return centred * factor, factor


def norm_back(grad, gain, normed, factor):
    scaled = grad * gain
    return factor * (
        scaled
        - jnp.mean(scaled, axis=-1, keepdims=True)
        - normed * jnp.mean(scaled * normed, axis=-1, keepdims=True)
    )


def precise(left, right):
    return jnp.dot(left, right, precision=lax.Precision.HIGH, preferred_element_type=f32)


def orthogonal_rows(own, oth, picks):
    gram = nt(own, own) + nt(oth, oth)
    eye = jnp.eye(gram.shape[0], dtype=f32)
    scale = 1.0 / (jnp.sqrt(jnp.sum(gram * eye)) + 1e-07)
    gram = gram * (scale * scale)
    polys = []
    for turn in range(4):
        square = precise(gram, gram)
        poly = coef_a * eye + coef_b * gram + coef_c * square
        polys.append(poly)
        half = coef_a * gram + coef_b * square + coef_c * precise(square, gram)
        gram = precise(poly, half)

    def take(arr):
        return jnp.concatenate([arr[start : start + count] for start, count in picks], axis=0)

    rows = take(gram)
    rows = coef_a * take(eye) + coef_b * rows + coef_c * precise(rows, gram)
    for poly in reversed(polys):
        rows = precise(rows, poly)
    return nn((rows * scale).astype(bf16), own)


def to_planes(blocks):
    bits = dp_bits()
    plane = lax.axis_index("dp") >> (bits - 2)
    got = []
    for far in range(4):
        block = lax.dynamic_index_in_dim(blocks, plane ^ far, 0, keepdims=False)
        got.append(swap_dp(block, far << (bits - 2)) if far else block)
    return jnp.stack(got)


def from_planes(outs):
    bits = dp_bits()
    plane = lax.axis_index("dp") >> (bits - 2)
    got = jnp.stack([swap_dp(outs[far], far << (bits - 2)) if far else outs[0] for far in range(4)])
    return [lax.dynamic_index_in_dim(got, plane ^ owner, 0, keepdims=False) for owner in range(4)]


def orthogonal_blocks(blocks):
    bits = dp_bits()
    rows = blocks.shape[1]
    cur = to_planes(blocks.astype(bf16))
    for b in range(bits - 3, 0, -1):
        cur = jnp.concatenate([cur, swap_dp(cur, 1 << b)], axis=1)
    cur = jnp.concatenate([cur, swap_dp(cur, 1)], axis=1)
    span = cur.shape[1]
    own = cur.reshape(4 * span, -1)
    oth = swap_tensor(own)
    picks = [(far * span, rows) for far in range(4)]
    out = orthogonal_rows(own, oth, picks).astype(bf16)
    return from_planes(out.reshape(4, rows, -1))


def per_device(
    tokens,
    lengths,
    live_count,
    cotangent,
    inflow,
    outflow,
    expand,
    shrink,
    emitter,
    inflow_prior,
    outflow_prior,
    expand_prior,
    shrink_prior,
    emitter_prior,
    vectors,
    vector_prior,
):
    side = lax.axis_index("tensor")
    place = lax.axis_index("dp")
    bits = dp_bits()
    entries_both = lengths.shape[1]
    entries = entries_both // 2
    rows = MICRO * entries * S
    half = inflow.shape[2]
    half_ff = expand.shape[1]
    half_out = emitter.shape[1]

    low_in = jnp.concatenate([inflow[0], inflow[1], inflow[2], outflow.T], axis=1).astype(bf16)
    view = (1,) + low_in.shape
    high = list(range(bits - 1, 1, -1))
    cur_in = gather_rows(low_in.reshape(view), high + ["x", 1, 0])
    low_rest = jnp.concatenate([expand, shrink.T, emitter], axis=1).astype(bf16)
    cur_rest = gather_rows(low_rest.reshape((1,) + low_rest.shape), high)
    cur_expand = gather_rows(cur_rest[..., :half_ff], [1, "x", 0])
    cur_shrink = gather_rows(cur_rest[..., half_ff : 2 * half_ff], ["x", 1, 0])
    cur_emit = gather_rows(cur_rest[..., 2 * half_ff :], [1, "x", 0])
    in_own, in_oth = halves_of(cur_in)
    qkv_w = (in_own[:, : 3 * half], in_oth[:, : 3 * half])
    out_w = (in_own[:, 3 * half :], in_oth[:, 3 * half :])
    expand_w = halves_of(cur_expand)
    shrink_w = halves_of(cur_shrink)
    emit_w = halves_of(cur_emit)

    gain_a = vectors[0:D]
    shift_a = vectors[D : 2 * D]
    gain_b = vectors[2 * D : 3 * D]
    shift_b = vectors[3 * D : 4 * D]
    bias_model = vectors[4 * D : 5 * D]

    def by_side(start, count):
        return [
            lax.dynamic_slice_in_dim(vectors, start + at * count, count) for at in (side, 1 - side)
        ]

    bias_hidden = by_side(5 * D, half_ff)
    bias_out = by_side(5 * D + FF, half_out)

    first_entry = side * entries
    x = lax.dynamic_slice_in_dim(tokens, first_entry * S, entries * S, 1).reshape(rows, D)
    x = x.astype(f32)
    length = lax.dynamic_slice_in_dim(lengths, first_entry, entries, 1).reshape(-1)
    cot_mine = lax.dynamic_slice_in_dim(cotangent, first_entry, entries, 1)
    cot_theirs = lax.dynamic_slice_in_dim(cotangent, entries - first_entry, entries, 1)
    cot_oth = swap_tensor(cot_theirs)
    entry_ids = place * entries_both + first_entry + jnp.arange(entries, dtype=jnp.int32)
    alive = (entry_ids[None, :] < live_count[:, None]).reshape(-1)
    cot = [
        jnp.where(alive[:, None], c.reshape(MICRO * entries, half_out), jnp.zeros((), bf16))
        for c in (cot_mine, cot_oth)
    ]
    live_slot = jnp.arange(S, dtype=jnp.int32)[None, :] < length[:, None]
    live_tiles = live_slot.astype(f32).reshape(rows // TILE, 1, TILE)
    slot_weight = live_slot.astype(f32) / length[:, None].astype(f32)

    normed_a, factor_a = norm_stats(x)
    act = (normed_a * gain_a + shift_a).astype(bf16)
    qkv = [nn(act, w).astype(bf16) for w in qkv_w]
    mixed = attend(live_tiles, qkv[0], qkv[1])
    hidden = x + (nt(mixed[0], out_w[0]) + nt(mixed[1], out_w[1]))
    normed_b, factor_b = norm_stats(hidden)
    act_two = (normed_b * gain_b + shift_b).astype(bf16)
    spread, slope = [], []
    for h in range(2):
        inner = nn(act_two, expand_w[h]) + bias_hidden[h]
        cdf = 0.5 * lax.erfc(inner * (-math.sqrt(0.5)))
        pdf = jnp.exp(-0.5 * inner * inner) * (1.0 / math.sqrt(2.0 * math.pi))
        spread.append((inner * cdf).astype(bf16))
        slope.append((cdf + inner * pdf).astype(bf16))
    result = hidden + (nt(spread[0], shrink_w[0]) + nt(spread[1], shrink_w[1]) + bias_model)
    pooled = jnp.sum(result.reshape(-1, S, D) * slot_weight[:, :, None], axis=1).astype(bf16)
    emitted = [(nn(pooled, emit_w[h]) + bias_out[h]).astype(bf16) for h in range(2)]

    grad_bias_out = [jnp.sum(c.astype(f32), axis=0) for c in cot]
    grad_emit = [tn(pooled, c).astype(bf16) for c in cot]
    shard_emit = reduce_chunk(grad_emit[0], grad_emit[1], [0, "x", 1] + high[::-1])
    d_pooled = nt(cot[0], emit_w[0]) + nt(cot[1], emit_w[1])
    d_result = (d_pooled[:, None, :] * slot_weight[:, :, None]).reshape(rows, D)
    d_result_low = d_result.astype(bf16)
    grad_bias_model = jnp.sum(d_result_low.astype(f32), axis=0)
    grad_shrink = [tn(d_result_low, f).astype(bf16) for f in spread]
    shard_shrink = reduce_chunk(grad_shrink[0], grad_shrink[1], [0, 1, "x"] + high[::-1])
    d_inner = [
        (nn(d_result_low, shrink_w[h]) * slope[h].astype(f32)).astype(bf16) for h in range(2)
    ]
    grad_bias_hidden = [jnp.sum(g.astype(f32), axis=0) for g in d_inner]
    grad_expand = [tn(act_two, g).astype(bf16) for g in d_inner]
    shard_expand = reduce_chunk(grad_expand[0], grad_expand[1], [0, "x", 1] + high[::-1])
    d_act_two = nt(d_inner[0], expand_w[0]) + nt(d_inner[1], expand_w[1])
    grad_gain_b = jnp.sum(d_act_two * normed_b, axis=0)
    grad_shift_b = jnp.sum(d_act_two, axis=0)
    d_hidden = d_result + norm_back(d_act_two, gain_b, normed_b, factor_b)
    d_hidden_low = d_hidden.astype(bf16)
    grad_out = [tn(d_hidden_low, m).astype(bf16) for m in mixed]
    d_mixed = [nn(d_hidden_low, w).astype(bf16) for w in out_w]
    d_qkv = attend_back(live_tiles, qkv[0], qkv[1], d_mixed[0], d_mixed[1])
    grad_in = [
        jnp.concatenate([tn(act, d_qkv[h]).astype(bf16), grad_out[h]], axis=1) for h in range(2)
    ]
    shard_in = reduce_chunk(grad_in[0], grad_in[1], [0, 1, "x"] + high[::-1])
    d_act = nt(d_qkv[0], qkv_w[0]) + nt(d_qkv[1], qkv_w[1])
    grad_gain_a = jnp.sum(d_act * normed_a, axis=0)
    grad_shift_a = jnp.sum(d_act, axis=0)
    token_grad = d_hidden + norm_back(d_act, gain_a, normed_a, factor_a)

    def both_sides(mine, theirs, cols):
        low = jnp.where(side == 0, mine, theirs)
        top = jnp.where(side == 0, theirs, mine)
        return jnp.concatenate(
            [low.reshape(MICRO, -1, cols), top.reshape(MICRO, -1, cols)], axis=1
        )

    emitted_all = both_sides(emitted[0], swap_tensor(emitted[1]), half_out)
    token_all = both_sides(token_grad, swap_tensor(token_grad.astype(bf16)).astype(f32), D)

    def placed(pair):
        low = jnp.where(side == 0, pair[0], pair[1])
        top = jnp.where(side == 0, pair[1], pair[0])
        return jnp.concatenate([low, top])

    vector_grad = jnp.concatenate(
        [
            grad_gain_a,
            grad_shift_a,
            grad_gain_b,
            grad_shift_b,
            grad_bias_model,
            placed(grad_bias_hidden),
            placed(grad_bias_out),
        ]
    )
    vector_total = sum_everywhere(vector_grad)

    shard_qkv = jnp.stack([shard_in[:, i * half : (i + 1) * half] for i in range(3)])
    inflow_velocity = 0.95 * inflow_prior + shard_qkv
    outflow_velocity = 0.95 * outflow_prior + shard_in[:, 3 * half :].T
    expand_velocity = 0.95 * expand_prior + shard_expand
    shrink_velocity = 0.95 * shrink_prior + shard_shrink.T
    emitter_velocity = 0.95 * emitter_prior + shard_emit
    wide = orthogonal_blocks(
        jnp.stack(
            [
                emitter_velocity,
                shrink_velocity.T,
                expand_velocity,
                jnp.zeros_like(expand_velocity),
            ]
        )
    )
    square = orthogonal_blocks(
        jnp.concatenate([inflow_velocity, outflow_velocity.T[None]], axis=0)
    )
    stretch = 0.6 * math.sqrt(FF / D)
    emitter_new = emitter - 0.6 * wide[0].astype(f32)
    shrink_new = shrink - stretch * wide[1].T.astype(f32)
    expand_new = expand - 0.6 * wide[2].astype(f32)
    inflow_new = inflow - 0.6 * jnp.stack(square[:3]).astype(f32)
    outflow_new = outflow - 0.6 * square[3].T.astype(f32)
    vector_velocity = 0.9 * vector_prior + vector_total
    vector_new = vectors - 0.005 * vector_velocity
    return (
        emitted_all,
        token_all,
        inflow_new,
        outflow_new,
        expand_new,
        shrink_new,
        emitter_new,
        inflow_velocity,
        outflow_velocity,
        expand_velocity,
        shrink_velocity,
        emitter_velocity,
        vector_new,
        vector_velocity,
    )


def solution(mesh):
    rows = P("dp", "tensor")
    cols = P("tensor", "dp")
    stacked = P(None, "dp", "tensor")
    placed = (
        P(None, "dp", None),
        P(None, "dp"),
        P(),
        stacked,
        stacked,
        cols,
        rows,
        cols,
        rows,
        stacked,
        cols,
        rows,
        cols,
        rows,
        P(),
        P(),
    )
    return jax.shard_map(
        per_device,
        mesh=mesh,
        in_specs=placed,
        out_specs=(
            stacked,
            P(None, "dp", None),
            stacked,
            cols,
            rows,
            cols,
            rows,
            stacked,
            cols,
            rows,
            cols,
            rows,
            P(),
            P(),
        ),
        check_vma=False,
    )
```
